32 devices in a mesh: groups: 2 (over y), dp: 4 (over z), expert: 2 (over core), cuts: 2 (over x).
Axes of the slice: x: 2, y: 2, z: 4, core: 2. Of those that a mesh axis runs over, the one named last changes fastest.
Arguments:
- tokens: bfloat16 [2048, 6144], P(('groups', 'dp', 'expert'), 'cuts'), parts along dimension 0, may hold values from -6 to 6
- routes: int32 [2048, 2], P(('groups', 'dp', 'expert')), parts along dimension 0, may hold values from 0 to 3, as said below
- gates: float32 [2048, 2], P(('groups', 'dp', 'expert')), parts along dimension 0, may hold values from 0.2 to 1
- w_gate: bfloat16 [4, 6144, 256], P('expert', None, 'cuts'), may hold values from -0.078125 to 0.078125
- w_up: bfloat16 [4, 6144, 256], P('expert', None, 'cuts'), may hold values from -0.078125 to 0.078125
- w_down: bfloat16 [4, 256, 6144], P('expert', 'cuts'), may hold values from -0.375 to 0.375
- cotangent: bfloat16 [2048, 6144], P(('groups', 'dp', 'expert'), 'cuts'), parts along dimension 0, may hold values from -0.59765625 to 0.59765625
Outputs:
- layer_out: bfloat16 [2048, 6144], P(('groups', 'dp', 'expert'), 'cuts'), parts along dimension 0
- token_grad: bfloat16 [2048, 6144], P(('groups', 'dp', 'expert'), 'cuts'), parts along dimension 0
- gate_grad: float32 [2048, 2], P(('groups', 'dp', 'expert')), parts along dimension 0
- grad_gate: float32 [8, 6144, 256], P(('groups', 'expert'), 'dp', 'cuts'), parts along dimension 0
- grad_up: float32 [8, 6144, 256], P(('groups', 'expert'), 'dp', 'cuts'), parts along dimension 0
- grad_down: float32 [8, 256, 6144], P(('groups', 'expert'), 'cuts', 'dp'), parts along dimension 0
The draws below stay inside these ranges and needn't reach their ends.
There are 2 independent parts, one for each index of `groups`. The reference program is written for one: setup_inputs(seed, part) draws one part's arguments, and reference() takes and returns one part's arrays. A program takes and returns all parts, laid end to end along the dimension named above; an argument that names none is the same for every part. Nothing has to cross between parts.
Inputs may be any that keep to these rules, and one draw needn't show every extreme that they name: `routes`: A token's two experts differ. Among the 128 tokens of one block (one index pair of dp and expert), no expert is named more than 72 times, and each of the 2 experts held at the block's own index of expert is named exactly 72 times.
All inputs are finite; a program needn't handle non-finite values.
Results may differ from the reference program's by a relative error of at most 0.0073.
Values may be sent and summed in bfloat16 or wider, within the bound.
A program may use at most 128 MiB of HBM per device.

```python
import jax
import jax.numpy as jnp
from jax import lax

D = 6144
EXP_DEV = 2
TOP = 2
TOK_DEV = 128
CAP = 72
EXPERTS = 4
FF = 256
TOKENS = 1024
N_EXPERT = 2
N_CUTS = 2


def draw_routes(key, part):
    key = jax.random.fold_in(key, 11)
    blocks = TOKENS // TOK_DEV
    remaining = TOP * TOK_DEV - EXP_DEV * CAP
    lowest = max(remaining - CAP, 0)
    highest = min(CAP, remaining)

    def one_block(block_index):
        block_key = jax.random.fold_in(key, block_index)
        key_count, key_flip, key_order = jax.random.split(block_key, 3)
        home = block_index % N_EXPERT
        first_remote = jax.random.randint(key_count, (), lowest, highest + 1).astype(jnp.int32)
        second_remote = remaining - first_remote
        full_cap = jnp.full((), CAP, jnp.int32)
        counts = jnp.where(home == 0, jnp.stack([full_cap, full_cap, first_remote, second_remote]), jnp.stack([first_remote, second_remote, full_cap, full_cap]))
        bounds = jnp.cumsum(counts)
        places = jnp.arange(TOP * TOK_DEV, dtype=jnp.int32)
        labels = jnp.sum((places[:, None] >= bounds[None, :3]).astype(jnp.int32), axis=1)
        pair_ids = jnp.stack([labels[:TOK_DEV], labels[TOK_DEV:]], axis=1)
        flips = jax.random.randint(key_flip, (TOK_DEV,), 0, 2)
        pair_ids = jnp.where(flips[:, None] == 1, pair_ids[:, ::-1], pair_ids)
        order = jax.random.permutation(key_order, TOK_DEV)
        return pair_ids[order]
    drawn = jax.vmap(one_block)(jnp.arange(blocks, dtype=jnp.int32))
    return drawn.reshape(TOKENS, TOP).astype(jnp.int32)


def raised(values, own_key, source, target, shards_of, factor):
    owner, partner = [(jnp.arange(values.shape[dim]) // (values.shape[dim] // shards_of)).reshape([-1 if axis == dim else 1 for axis in range(values.ndim)]) for dim in (source, target)]
    chosen = jax.random.permutation(own_key, shards_of)[partner]
    strong = (owner == chosen) | (owner == (partner + shards_of // 2) % shards_of)
    return jnp.where(strong, factor * values, values)


def shard_levels(stream_key, shape, shards, smallest, largest):
    def one(axis_at, shards_of):
        draws = jax.random.uniform(jax.random.fold_in(jax.random.fold_in(stream_key, 6), axis_at), (shards_of,), jnp.float32, smallest / len(shards), largest / len(shards))
        return jnp.repeat(jnp.exp(draws), shape[axis_at] // shards_of).reshape((-1,) + (1,) * (len(shape) - axis_at - 1))

    loudness = one(*shards[0])
    for cut in shards[1:]:
        loudness = loudness * one(*cut)
    return loudness


def gaussian(rng, extent, scale, bound, pieces=(), kind=jnp.bfloat16):
    level = shard_levels(rng, extent, pieces, -0.22, 0.18) if pieces else 1.0
    result = jax.random.normal(rng, extent, jnp.float32) * scale * level
    return jnp.minimum(jnp.maximum(result, -bound), bound).astype(kind)


def noise_with(key, extent, spread, most, cuts, heavy, kind=jnp.bfloat16):
    values = spread * jax.random.normal(key, extent, jnp.float32)
    if cuts:
        values = values * shard_levels(key, extent, cuts, -0.22, 0.18)
    return jnp.clip(raised(values, jax.random.fold_in(key, 3), *heavy), -most, most).astype(kind)


def setup_inputs(seed: int = 0, part: int = 0) -> dict:
    key_list = jax.random.split(jax.random.key(seed), 8)
    part_keys = jax.random.split(jax.random.fold_in(key_list[7], part), 8)
    tokens = noise_with(part_keys[0], (TOKENS, D), 1.0, 6.0, ((0, 8), (1, 2)), (0, 1, 8, 2.0))
    routes = draw_routes(jax.random.fold_in(jax.random.fold_in(key_list[7], part), 71), part)
    gates = jnp.clip(0.2 + 0.8 * jax.random.uniform(part_keys[2], (TOKENS, TOP), jnp.float32) ** shard_levels(part_keys[2], (TOKENS, TOP), ((0, 8),), -0.2, 0.2), 0.2, 1.0)
    w_gate = gaussian(key_list[3], (EXPERTS, D, FF), D ** -0.5, 0.078125, ((0, 2), (2, 2)))
    w_up = gaussian(key_list[4], (EXPERTS, D, FF), D ** -0.5, 0.078125, ((0, 2), (2, 2)))
    w_down = gaussian(key_list[5], (EXPERTS, FF, D), FF ** -0.5, 0.375, ((0, 2), (1, 2)))
    cotangent = gaussian(part_keys[6], (TOKENS, D), 0.1, 0.59765625, ((0, 8), (1, 2)))
    return dict(tokens=tokens, routes=routes, gates=gates, w_gate=w_gate, w_up=w_up, w_down=w_down, cotangent=cotangent)


def expert_pass(operands):
    expert_rows, dout_rows, gate_weight, up_weight, down_weight = operands
    gate_act = jnp.dot(expert_rows, gate_weight, preferred_element_type=jnp.float32)
    up_act = jnp.dot(expert_rows, up_weight, preferred_element_type=jnp.float32)
    sigma = jax.nn.sigmoid(gate_act)
    silu_act = gate_act * sigma
    hidden = (silu_act * up_act).astype(jnp.bfloat16)
    d_hidden = jnp.dot(dout_rows, down_weight.T, preferred_element_type=jnp.float32)
    d_gate = (d_hidden * up_act * sigma * (1.0 + gate_act * (1.0 - sigma))).astype(jnp.bfloat16)
    d_up = (d_hidden * silu_act).astype(jnp.bfloat16)
    width = FF // N_CUTS
    out_total = jnp.zeros((expert_rows.shape[0], D), jnp.float32)
    grad_total = jnp.zeros((expert_rows.shape[0], D), jnp.float32)
    for cut_index in range(N_CUTS):
        low = cut_index * width
        high = low + width
        out_piece = jnp.dot(hidden[:, low:high], down_weight[low:high], preferred_element_type=jnp.float32)
        out_total = out_total + lax.optimization_barrier(out_piece.astype(jnp.bfloat16)).astype(jnp.float32)
        grad_piece = jnp.dot(d_gate[:, low:high], gate_weight[:, low:high].T, preferred_element_type=jnp.float32)
        grad_piece = grad_piece + jnp.dot(d_up[:, low:high], up_weight[:, low:high].T, preferred_element_type=jnp.float32)
        grad_total = grad_total + lax.optimization_barrier(grad_piece.astype(jnp.bfloat16)).astype(jnp.float32)
    grad_gate = jnp.dot(expert_rows.T, d_gate, preferred_element_type=jnp.float32)
    grad_up = jnp.dot(expert_rows.T, d_up, preferred_element_type=jnp.float32)
    grad_down = jnp.dot(hidden.T, dout_rows, preferred_element_type=jnp.float32)
    return out_total.astype(jnp.bfloat16), grad_total.astype(jnp.bfloat16), grad_gate, grad_up, grad_down


def reference(tokens, routes, gates, w_gate, w_up, w_down, cotangent):
    experts = w_gate.shape[0]
    blocks = TOKENS // TOK_DEV
    pair_ids = routes.reshape(blocks, TOK_DEV * 2)
    onehot = (pair_ids[:, :, None] == jnp.arange(experts, dtype=jnp.int32)[None, None, :]).astype(jnp.int32)
    running = jnp.cumsum(onehot, axis=1)
    position = jnp.sum(onehot * (running - 1), axis=2)
    pair_slot = (pair_ids * CAP + position).astype(jnp.int32)
    block_ids = jnp.arange(blocks, dtype=jnp.int32)[:, None]
    token_ids = (block_ids * TOK_DEV + jnp.arange(TOK_DEV * 2, dtype=jnp.int32)[None, :] // 2).astype(jnp.int32)
    slot_token = jnp.full((blocks, experts * CAP), -1, jnp.int32).at[block_ids, pair_slot].set(token_ids)
    slot_weight = jnp.zeros((blocks, experts * CAP), jnp.float32).at[block_ids, pair_slot].set(gates.reshape(blocks, TOK_DEV * 2).astype(jnp.float32))
    valid = slot_token >= 0
    safe_token = jnp.maximum(slot_token, 0)
    slot_x = jnp.where(valid[:, :, None], tokens[safe_token], jnp.zeros((), tokens.dtype))
    slot_dout = (slot_weight[:, :, None] * cotangent[safe_token].astype(jnp.float32)).astype(jnp.bfloat16)
    by_expert_x = slot_x.reshape(blocks, experts, CAP, D).transpose(1, 0, 2, 3).reshape(experts, blocks * CAP, D)
    by_expert_d = slot_dout.reshape(blocks, experts, CAP, D).transpose(1, 0, 2, 3).reshape(experts, blocks * CAP, D)
    slot_out, slot_dx, grad_gate, grad_up, grad_down = lax.map(expert_pass, (by_expert_x, by_expert_d, w_gate, w_up, w_down))
    slot_out = slot_out.reshape(experts, blocks, CAP, D).transpose(1, 0, 2, 3).reshape(blocks, experts * CAP, D)
    slot_dx = slot_dx.reshape(experts, blocks, CAP, D).transpose(1, 0, 2, 3).reshape(blocks, experts * CAP, D)
    first_slot = pair_slot[:, 0::2]
    second_slot = pair_slot[:, 1::2]
    out_first = slot_out[block_ids, first_slot].reshape(TOKENS, D).astype(jnp.float32)
    out_second = slot_out[block_ids, second_slot].reshape(TOKENS, D).astype(jnp.float32)
    gates_f = gates.astype(jnp.float32)
    layer_out = (gates_f[:, 0:1] * out_first + gates_f[:, 1:2] * out_second).astype(jnp.bfloat16)
    dx_first = slot_dx[block_ids, first_slot].reshape(TOKENS, D).astype(jnp.float32)
    dx_second = slot_dx[block_ids, second_slot].reshape(TOKENS, D).astype(jnp.float32)
    token_grad = (dx_first + dx_second).astype(jnp.bfloat16)
    cot_f = cotangent.astype(jnp.float32)
    gate_grad = jnp.stack([jnp.sum(cot_f * out_first, axis=1), jnp.sum(cot_f * out_second, axis=1)], axis=1)
    return layer_out, token_grad, gate_grad, grad_gate, grad_up, grad_down
```

```python
import functools

import jax
import jax.numpy as jnp
from jax import lax
from jax.experimental import pallas as pl
from jax.experimental.pallas import tpu as pltpu
from jax.sharding import PartitionSpec as P

MESH = pl.DeviceIdType.MESH
BF = jnp.bfloat16
F32 = jnp.float32


def dot(a, b, ca, cb):
    return lax.dot_general(a, b, (((ca,), (cb,)), ((), ())), preferred_element_type=F32)


def tile_of(width):
    for tile in (512, 384, 256, 128):
        if width % tile == 0:
            return tile
    return width


def kernel(
    N, C, tok, cot, aux_own, aux_oth, wg, wu, wd_in,
    out_o, grad_o, gg_o, g_gate, g_up, g_down,
    wgu, wd, xg, zr, hz, aux, acc, accd, hid, ploc, csend, cr, xsend, xr, ggs, ggr, hwt,
    wsem, osem, xs_s, xs_r, co_s, co_r, au_s, au_r, z_s, z_r, zl, f_s, f_r,
    h_s, h_r, rc_s, rc_r, rx_s, rx_r, gg_s, gg_r,
):
    d, e, c = lax.axis_index("dp"), lax.axis_index("expert"), lax.axis_index("cuts")
    other = 1 - e
    rows = tok.shape[0]
    R = N // C
    Dq = tok.shape[1] // R
    ins = (tok, cot)
    K = wg.shape[0]
    W = wg.shape[2]

    def rel(i):
        return lax.rem(c + i, C)

    def quarter(p):
        return rel(p // R) * R + p % R

    def cols(p):
        return pl.ds(pl.multiple_of(quarter(p) * Dq, 128), Dq)

    def rcopy(src, dst, ss, rs, dev):
        return pltpu.make_async_remote_copy(
            src_ref=src, dst_ref=dst, send_sem=ss, recv_sem=rs, device_id=dev, device_id_type=MESH
        )

    barrier = pltpu.get_barrier_semaphore()
    peers = [{"cuts": rel(i)} for i in range(1, C)]
    peers += [{"expert": other, "cuts": rel(i)} for i in range(C)]
    peers += [{"dp": lax.rem(d + i, N)} for i in range(1, N)]
    for peer in peers:
        pl.semaphore_signal(barrier, inc=1, device_id=peer, device_id_type=MESH)
    pl.semaphore_wait(barrier, len(peers))

    own = pl.ds(0, rows)
    oth = pl.ds(rows, rows)
    core = {"expert": other}

    x_out = []
    c_out = []
    loc = []
    aux_copy = rcopy(aux_oth, aux.at[1], au_s, au_r, core)
    aux_copy.start()
    aux_loc = pltpu.make_async_copy(aux_own, aux.at[0], wsem.at[2 * K + 1])
    aux_loc.start()
    for kind in range(2):
        for r in range(R):
            src = ins[kind].at[:, pl.ds(r * Dq, Dq)]
            for i in range(1, C):
                p = (C - i) * R + r
                cp = rcopy(src, xg.at[kind, p, own], xs_s.at[kind, p], xs_r.at[kind, p], {"cuts": rel(i)})
                cp.start()
                x_out.append(cp)
            cp = rcopy(src, xg.at[kind, r, oth], co_s.at[kind, r], co_r.at[kind, r], core)
            cp.start()
            c_out.append(cp)
            cp = pltpu.make_async_copy(src, xg.at[kind, r, own], osem.at[kind, r])
            cp.start()
            loc.append(cp)
    w_loads = []
    for k in range(K):
        for j, w in enumerate((wg, wu)):
            cp = pltpu.make_async_copy(
                w.at[k], wgu.at[:, pl.ds((2 * k + j) * W, W)], wsem.at[2 * k + j]
            )
            cp.start()
            w_loads.append(cp)
    wd_load = pltpu.make_async_copy(wd_in, wd, wsem.at[2 * K])
    wd_load.start()

    def z_copy(kind, p):
        q = quarter(p)
        return rcopy(
            xg.at[kind, p, own], zr.at[kind, d, own], z_s.at[kind, p], z_r.at[kind, d], {"dp": q}
        )

    def z_local(kind, p):
        return pltpu.make_async_copy(xg.at[kind, p], zr.at[kind, d], zl.at[kind])

    def arrive(kind, p):
        if p < R:
            loc[kind * R + p].wait()
        else:
            rcopy(
                xg.at[kind, p, own], xg.at[kind, p, own], xs_s.at[kind, p], xs_r.at[kind, p],
                {"cuts": c},
            ).wait_recv()
            cp = rcopy(
                xg.at[kind, p, own], xg.at[kind, p, oth], co_s.at[kind, p], co_r.at[kind, p], core
            )
            cp.start()
            c_out.append(cp)

        @pl.when(quarter(p) != d)
        def _():
            z_copy(kind, p).start()

        rcopy(
            xg.at[kind, p, own], xg.at[kind, p, oth], co_s.at[kind, p], co_r.at[kind, p], core
        ).wait_recv()

        @pl.when(quarter(p) == d)
        def _():
            z_local(kind, p).start()

    acc[...] = jnp.zeros_like(acc)
    accd[...] = jnp.zeros_like(accd)
    for cp in w_loads:
        cp.wait()
    for p in range(N):
        arrive(0, p)
        acc[...] += dot(xg[0, p], wgu[cols(p), :], 1, 0)
    aux_copy.wait()
    aux_loc.wait()
    wd_load.wait()

    def weight(k):
        return jnp.concatenate([aux[0, :, k : k + 1], aux[1, :, k : k + 1]], axis=0)

    for k in range(K):
        gs = pl.ds(2 * k * W, W)
        us = pl.ds((2 * k + 1) * W, W)
        g = acc[:, gs]
        u = acc[:, us]
        s = jax.nn.sigmoid(g)
        silu = g * s
        h = silu * u
        w = weight(k)
        hid[:, pl.ds(k * W, W)] = h
        hz[d, :, pl.ds((2 * K + k) * W, W)] = (h * w).astype(BF)
        acc[:, gs] = u * s * (1.0 + g * (1.0 - s)) * w
        acc[:, us] = silu * w

    tile = tile_of(Dq)
    rx_out = []
    rc_out = []

    def back(kind):
        order = list(range(R, N)) + list(range(R))
        for p in order:
            base = quarter(p) * Dq

            def step(t, _, p=p, base=base):
                at = pl.ds(pl.multiple_of(t * tile, 128), tile)
                wat = pl.ds(pl.multiple_of(base + t * tile, 128), tile)
                if kind == 0:
                    part = dot(hz[d, :, pl.ds(2 * K * W, K * W)], wd[:, wat], 1, 0)
                else:
                    part = dot(hz[d, :, pl.ds(0, 2 * K * W)], wgu[wat, :], 1, 1)
                ploc[kind, p, :, at] = part[:rows]
                csend[kind, p, :, at] = part[rows:].astype(BF)
                return 0

            lax.fori_loop(0, Dq // tile, step, 0)
            cp = rcopy(csend.at[kind, p], cr.at[kind, p], rc_s.at[kind, p], rc_r.at[kind, p], core)
            cp.start()
            rc_out.append(cp)
        for p in order[: N - R]:
            rcopy(
                csend.at[kind, p], cr.at[kind, p], rc_s.at[kind, p], rc_r.at[kind, p], core
            ).wait_recv()
            xsend[kind, p - R] = (ploc[kind, p] + cr[kind, p].astype(F32)).astype(BF)
            cp = rcopy(
                xsend.at[kind, p - R], xr.at[kind, p - R], rx_s.at[kind, p - R],
                rx_r.at[kind, p - R], {"cuts": rel(p // R)},
            )
            cp.start()
            rx_out.append(cp)

    back(0)

    for p in range(N):
        arrive(1, p)
        accd[...] += dot(xg[1, p], wd[:, cols(p)], 1, 1)

    ggs[...] = jnp.zeros_like(ggs)
    for k in range(K):
        dh = accd[:, pl.ds(k * W, W)]
        prod = hid[:, pl.ds(k * W, W)] * dh
        for slot in range(2):
            piece = prod[slot * rows : (slot + 1) * rows]
            ggs[slot, pl.ds(k, 1), :] = jnp.sum(piece.T, axis=0, keepdims=True)
        hz[d, :, pl.ds(2 * k * W, W)] = (acc[:, pl.ds(2 * k * W, W)] * dh).astype(BF)
        hz[d, :, pl.ds((2 * k + 1) * W, W)] = (acc[:, pl.ds((2 * k + 1) * W, W)] * dh).astype(BF)

    gg_out = []
    for i in range(C):
        for slot in range(2):
            if i == 0 and slot == 0:
                continue
            dev = {"cuts": rel(i)} if slot == 0 else {"expert": other, "cuts": rel(i)}
            cp = rcopy(ggs.at[slot], ggr.at[slot, i], gg_s.at[slot, i], gg_r.at[slot, i], dev)
            cp.start()
            gg_out.append(cp)
    ggr[0, 0] = ggs[0]

    h_out = []
    for i in range(1, N):
        cp = rcopy(hz.at[d], hz.at[d], h_s.at[i], h_r.at[d], {"dp": lax.rem(d + i, N)})
        cp.start()
        h_out.append(cp)

    back(1)

    f_out = []
    for kind in range(2):
        for i in range(1, N):
            ds = lax.rem(d + i, N)
            z = zr.at[kind, ds, own]
            rcopy(z, z, z_s.at[kind, i], z_r.at[kind, ds], {"dp": d}).wait_recv()
            cp = rcopy(z, zr.at[kind, ds, oth], f_s.at[kind, ds], f_r.at[kind, ds], core)
            cp.start()
            f_out.append(cp)
    for i in range(1, N):
        ds = lax.rem(d + i, N)
        rcopy(hz.at[ds], hz.at[ds], h_s.at[i], h_r.at[ds], {"dp": d}).wait_recv()
    for kind in range(2):
        z_local(kind, 0).wait()
        for i in range(1, N):
            ds = lax.rem(d + i, N)
            z = zr.at[kind, ds, oth]
            rcopy(z, z, f_s.at[kind, ds], f_r.at[kind, ds], core).wait_recv()

    flat = N * 2 * rows
    hwt[...] = hz[:, :, pl.ds(2 * K * W, K * W)].reshape(flat, K * W).T
    wt = 256 if Dq % 256 == 0 else 128

    def wstep(t, _):
        at = pl.ds(pl.multiple_of(t * wt, 128), wt)
        full = dot(
            zr[0, :, :, at].reshape(flat, wt), hz[:, :, pl.ds(0, 2 * K * W)].reshape(flat, 2 * K * W), 0, 0
        )
        down = dot(hwt[...], zr[1, :, :, at].reshape(flat, wt), 1, 0)
        for k in range(K):
            g_gate[k, at, :] = full[:, 2 * k * W : (2 * k + 1) * W]
            g_up[k, at, :] = full[:, (2 * k + 1) * W : (2 * k + 2) * W]
            g_down[k, :, at] = down[k * W : (k + 1) * W]
        return 0

    lax.fori_loop(0, Dq // wt, wstep, 0)

    outs = (out_o, grad_o)
    for kind in range(2):
        for r in range(R):
            rcopy(
                csend.at[kind, r], cr.at[kind, r], rc_s.at[kind, r], rc_r.at[kind, r], core
            ).wait_recv()
            total = ploc[kind, r] + cr[kind, r].astype(F32)
            for i in range(1, C):
                n = (i - 1) * R + r
                rcopy(
                    xr.at[kind, n], xr.at[kind, n], rx_s.at[kind, n], rx_r.at[kind, n], {"cuts": c}
                ).wait_recv()
                total = total + xr[kind, n].astype(F32)
            outs[kind][:, pl.ds(r * Dq, Dq)] = total.astype(BF)

    for i in range(C):
        for slot in range(2):
            if i or slot:
                g = ggr.at[slot, i]
                rcopy(g, g, gg_s.at[slot, i], gg_r.at[slot, i], {"cuts": c}).wait_recv()
    gg_o[...] = jnp.sum(ggr[...], axis=1)

    for cp in x_out + c_out + rc_out + rx_out + gg_out + h_out + f_out:
        cp.wait_send()
    for kind in range(2):
        for p in range(N):
            @pl.when(quarter(p) != d)
            def _():
                z_copy(kind, p).wait_send()


def on_device(N, C, tokens, routes, gates, w_gate, w_up, w_down, cotangent):
    K, D, W = w_gate.shape
    rows, Dc = tokens.shape
    R = N // C
    Dq = Dc // R
    e = lax.axis_index("expert")
    lanes = jnp.arange(128, dtype=jnp.int32)
    onehot = (routes[:, :, None] == lanes[None, None, :]) & (lanes < 2 * K)[None, None, :]
    dense = jnp.sum(jnp.where(onehot, gates[:, :, None], 0.0), axis=1)
    low, high = dense, jnp.roll(dense, -K, axis=1)
    aux_own = jnp.where(e == 0, low, high)
    aux_oth = jnp.where(e == 0, high, low)
    DMA = pltpu.SemaphoreType.DMA
    V = pltpu.VMEM
    rows2 = 2 * rows
    vm = pl.BlockSpec(memory_space=pltpu.VMEM)
    hb = pl.BlockSpec(memory_space=pl.ANY)
    out, grad, gg, gg_gate, gg_up, gg_down = pl.pallas_call(
        functools.partial(kernel, N, C),
        out_shape=(
            jax.ShapeDtypeStruct((rows, Dc), BF),
            jax.ShapeDtypeStruct((rows, Dc), BF),
            jax.ShapeDtypeStruct((2, 8, 128), F32),
            jax.ShapeDtypeStruct((K, Dq, W), F32),
            jax.ShapeDtypeStruct((K, Dq, W), F32),
            jax.ShapeDtypeStruct((K, W, Dq), F32),
        ),
        in_specs=[hb] * 7,
        out_specs=(vm,) * 6,
        scratch_shapes=[
            V((D, 2 * K * W), BF),
            V((K * W, D), BF),
            V((2, N, rows2, Dq), BF),
            V((2, N, rows2, Dq), BF),
            V((N, rows2, 3 * K * W), BF),
            V((2, rows, 128), F32),
            V((rows2, 2 * K * W), F32),
            V((rows2, K * W), F32),
            V((rows2, K * W), F32),
            V((2, N, rows, Dq), F32),
            V((2, N, rows, Dq), BF),
            V((2, N, rows, Dq), BF),
            V((2, N - R, rows, Dq), BF),
            V((2, N - R, rows, Dq), BF),
            V((2, 8, 128), F32),
            V((2, C, 8, 128), F32),
            V((K * W, N * rows2), BF),
            DMA((2 * K + 2,)),
            DMA((2, R)),
            DMA((2, N)),
            DMA((2, N)),
            DMA((2, N)),
            DMA((2, N)),
            DMA,
            DMA,
            DMA((2, N)),
            DMA((2, N)),
            DMA((2,)),
            DMA((2, N)),
            DMA((2, N)),
            DMA((N,)),
            DMA((N,)),
            DMA((2, N)),
            DMA((2, N)),
            DMA((2, N - R)),
            DMA((2, N - R)),
            DMA((2, C)),
            DMA((2, C)),
        ],
        compiler_params=pltpu.CompilerParams(
            collective_id=0, has_side_effects=True, vmem_limit_bytes=62 * 2**20
        ),
    )(
        tokens, cotangent, aux_own, aux_oth, w_gate, w_up, w_down.reshape(K * W, D)
    )
    mine = gg[0, :K].T
    theirs = gg[1, :K].T
    table = jnp.where(
        e == 0, jnp.concatenate([mine, theirs], 1), jnp.concatenate([theirs, mine], 1)
    )
    hot = routes[:, :, None] == jnp.arange(2 * K, dtype=jnp.int32)[None, None, :]
    gate_grad = jnp.sum(jnp.where(hot, table[:, None, :], 0.0), axis=2)
    return (out, grad, gate_grad, gg_gate, gg_up, gg_down)


def solution(mesh):
    in_specs = (
        P(("groups", "dp", "expert"), "cuts"),
        P(("groups", "dp", "expert"), None),
        P(("groups", "dp", "expert"), None),
        P("expert", None, "cuts"),
        P("expert", None, "cuts"),
        P("expert", "cuts", None),
        P(("groups", "dp", "expert"), "cuts"),
    )
    out_specs = (
        P(("groups", "dp", "expert"), "cuts"),
        P(("groups", "dp", "expert"), "cuts"),
        P(("groups", "dp", "expert"), None),
        P(("groups", "expert"), "dp", "cuts"),
        P(("groups", "expert"), "dp", "cuts"),
        P(("groups", "expert"), "cuts", "dp"),
    )
    return jax.shard_map(
        functools.partial(on_device, mesh.shape["dp"], mesh.shape["cuts"]),
        mesh=mesh, in_specs=in_specs, out_specs=out_specs, check_vma=False,
    )
```

```python
import functools

import jax
import jax.numpy as jnp
from jax import lax
from jax.experimental import pallas as pl
from jax.experimental.pallas import tpu as pltpu
from jax.sharding import PartitionSpec as P

MESH = pl.DeviceIdType.MESH
BF = jnp.bfloat16
F32 = jnp.float32


def dot(a, b, ca, cb):
    return lax.dot_general(a, b, (((ca,), (cb,)), ((), ())), preferred_element_type=F32)


def tile_of(width):
    for tile in (512, 384, 256, 128):
        if width % tile == 0:
            return tile
    return width


def kernel(
    N, C, tok, cot, aux_own, aux_oth, wg, wu, wd_in,
    out_o, grad_o, gg_o, g_gate, g_up, g_down,
    wgu, wd, xg, zr, hz, aux, acc, accd, hid, ploc, csend, cr, xsend, xr, ggs, ggr, hwt,
    wsem, osem, xs_s, xs_r, co_s, co_r, au_s, au_r, z_s, z_r, zl, f_s, f_r,
    f1_s, f1_r, xf_s, xf_r, h_s, h_r, rc_s, rc_r, rx_s, rx_r, gg_s, gg_r,
):
    d, e, c = lax.axis_index("dp"), lax.axis_index("expert"), lax.axis_index("cuts")
    other = 1 - e
    rows = tok.shape[0]
    R = N // C
    Dq = tok.shape[1] // R
    ins = (tok, cot)
    K = wg.shape[0]
    W = wg.shape[2]

    def rel(i):
        return lax.rem(c + i, C)

    def quarter(p):
        return rel(p // R) * R + p % R

    def cols(p):
        return pl.ds(pl.multiple_of(quarter(p) * Dq, 128), Dq)

    def rcopy(src, dst, ss, rs, dev):
        return pltpu.make_async_remote_copy(
            src_ref=src, dst_ref=dst, send_sem=ss, recv_sem=rs, device_id=dev, device_id_type=MESH
        )

    barrier = pltpu.get_barrier_semaphore()
    peers = [{"cuts": rel(i)} for i in range(1, C)]
    peers += [{"expert": other, "cuts": rel(i)} for i in range(C)]
    peers += [{"dp": lax.rem(d + i, N)} for i in range(1, N)]
    for peer in peers:
        pl.semaphore_signal(barrier, inc=1, device_id=peer, device_id_type=MESH)
    pl.semaphore_wait(barrier, len(peers))

    own = pl.ds(0, rows)
    oth = pl.ds(rows, rows)
    core = {"expert": other}

    x_out = []
    c_out = []
    loc = []
    aux_copy = rcopy(aux_oth, aux.at[1], au_s, au_r, core)
    aux_copy.start()
    aux_loc = pltpu.make_async_copy(aux_own, aux.at[0], wsem.at[2 * K + 1])
    aux_loc.start()
    for kind in range(2):
        for r in range(R):
            src = ins[kind].at[:, pl.ds(r * Dq, Dq)]
            for i in range(1, C):
                p = (C - i) * R + r
                cp = rcopy(src, xg.at[kind, p, own], xs_s.at[kind, p], xs_r.at[kind, p], {"cuts": rel(i)})
                cp.start()
                x_out.append(cp)
            cp = rcopy(src, xg.at[kind, r, oth], co_s.at[kind, r], co_r.at[kind, r], core)
            cp.start()
            c_out.append(cp)
            cp = pltpu.make_async_copy(src, xg.at[kind, r, own], osem.at[kind, r])
            cp.start()
            loc.append(cp)
    w_loads = []
    for k in range(K):
        for j, w in enumerate((wg, wu)):
            cp = pltpu.make_async_copy(
                w.at[k], wgu.at[:, pl.ds((2 * k + j) * W, W)], wsem.at[2 * k + j]
            )
            cp.start()
            w_loads.append(cp)
    wd_load = pltpu.make_async_copy(wd_in, wd, wsem.at[2 * K])
    wd_load.start()

    hr = rows // C

    def share(slot, cc):
        return pl.ds(pl.multiple_of(slot * rows + cc * hr, 16), hr)

    def z_copy(kind, p):
        part = own if kind == 0 else share(0, c)
        return rcopy(
            xg.at[kind, p, part], zr.at[kind, d, part], z_s.at[kind, p], z_r.at[kind, d],
            {"dp": quarter(p)},
        )

    def z_local(kind, p):
        return pltpu.make_async_copy(xg.at[kind, p], zr.at[kind, d], zl.at[kind])

    def z_start(kind, p):
        @pl.when(quarter(p) != d)
        def _():
            z_copy(kind, p).start()

    def arrive(kind, p):
        if p >= R:
            rcopy(
                xg.at[kind, p, own], xg.at[kind, p, own], xs_s.at[kind, p], xs_r.at[kind, p],
                {"cuts": c},
            ).wait_recv()
            cp = rcopy(
                xg.at[kind, p, own], xg.at[kind, p, oth], co_s.at[kind, p], co_r.at[kind, p], core
            )
            cp.start()
            c_out.append(cp)
            z_start(kind, p)
        rcopy(
            xg.at[kind, p, own], xg.at[kind, p, oth], co_s.at[kind, p], co_r.at[kind, p], core
        ).wait_recv()

        @pl.when(quarter(p) == d)
        def _():
            z_local(kind, p).start()

    acc[...] = jnp.zeros_like(acc)
    accd[...] = jnp.zeros_like(accd)
    for kind in range(2):
        for p in range(R):
            loc[kind * R + p].wait()
            z_start(kind, p)
    for p in range(N):
        arrive(0, p)
        if p == 0:
            for cp in w_loads:
                cp.wait()
        acc[...] += dot(xg[0, p], wgu[cols(p), :], 1, 0)
    aux_copy.wait()
    aux_loc.wait()
    wd_load.wait()

    def weight(k):
        return jnp.concatenate([aux[0, :, k : k + 1], aux[1, :, k : k + 1]], axis=0)

    for k in range(K):
        gs = pl.ds(2 * k * W, W)
        us = pl.ds((2 * k + 1) * W, W)
        g = acc[:, gs]
        u = acc[:, us]
        s = jax.nn.sigmoid(g)
        silu = g * s
        h = silu * u
        w = weight(k)
        hid[:, pl.ds(k * W, W)] = h
        hz[d, :, pl.ds((2 * K + k) * W, W)] = (h * w).astype(BF)
        acc[:, gs] = u * s * (1.0 + g * (1.0 - s)) * w
        acc[:, us] = silu * w

    tile = tile_of(Dq)
    rx_out = []
    rc_out = []

    def back(kind):
        order = list(range(R, N)) + list(range(R))
        for p in order:
            base = quarter(p) * Dq

            def step(t, _, p=p, base=base):
                at = pl.ds(pl.multiple_of(t * tile, 128), tile)
                wat = pl.ds(pl.multiple_of(base + t * tile, 128), tile)
                if kind == 0:
                    part = dot(hz[d, :, pl.ds(2 * K * W, K * W)], wd[:, wat], 1, 0)
                else:
                    part = dot(hz[d, :, pl.ds(0, 2 * K * W)], wgu[wat, :], 1, 1)
                ploc[kind, p, :, at] = part[:rows]
                csend[kind, p, :, at] = part[rows:].astype(BF)
                return 0

            lax.fori_loop(0, Dq // tile, step, 0)
            cp = rcopy(csend.at[kind, p], cr.at[kind, p], rc_s.at[kind, p], rc_r.at[kind, p], core)
            cp.start()
            rc_out.append(cp)
        for p in order[: N - R]:
            rcopy(
                csend.at[kind, p], cr.at[kind, p], rc_s.at[kind, p], rc_r.at[kind, p], core
            ).wait_recv()
            xsend[kind, p - R] = (ploc[kind, p] + cr[kind, p].astype(F32)).astype(BF)
            cp = rcopy(
                xsend.at[kind, p - R], xr.at[kind, p - R], rx_s.at[kind, p - R],
                rx_r.at[kind, p - R], {"cuts": rel(p // R)},
            )
            cp.start()
            rx_out.append(cp)

    back(0)

    for p in range(N):
        arrive(1, p)
        accd[...] += dot(xg[1, p], wd[:, cols(p)], 1, 1)

    ggs[...] = jnp.zeros_like(ggs)
    for k in range(K):
        dh = accd[:, pl.ds(k * W, W)]
        prod = hid[:, pl.ds(k * W, W)] * dh
        for slot in range(2):
            piece = prod[slot * rows : (slot + 1) * rows]
            ggs[slot, pl.ds(k, 1), :] = jnp.sum(piece.T, axis=0, keepdims=True)
        hz[d, :, pl.ds(2 * k * W, W)] = (acc[:, pl.ds(2 * k * W, W)] * dh).astype(BF)
        hz[d, :, pl.ds((2 * k + 1) * W, W)] = (acc[:, pl.ds((2 * k + 1) * W, W)] * dh).astype(BF)

    gg_out = []
    for i in range(C):
        for slot in range(2):
            if i == 0 and slot == 0:
                continue
            dev = {"cuts": rel(i)} if slot == 0 else {"expert": other, "cuts": rel(i)}
            cp = rcopy(ggs.at[slot], ggr.at[slot, i], gg_s.at[slot, i], gg_r.at[slot, i], dev)
            cp.start()
            gg_out.append(cp)
    ggr[0, 0] = ggs[0]

    pieces = (own, oth)

    def h_copy(ds, n, up):
        at = hz.at[ds, pieces[n]]
        to = jnp.minimum(d + 1, N - 1) if up else jnp.maximum(d - 1, 0)
        return rcopy(at, at, h_s.at[int(up), ds, n], h_r.at[ds, n], {"dp": to})

    for n in range(2):
        @pl.when(d < N - 1)
        def _():
            h_copy(d, n, True).start()

        @pl.when(d > 0)
        def _():
            h_copy(d, n, False).start()

    back(1)

    f_out = []
    for i in range(1, N):
        ds = lax.rem(d + i, N)
        z = zr.at[0, ds, own]
        rcopy(z, z, z_s.at[0, i], z_r.at[0, ds], {"dp": d}).wait_recv()
        cp = rcopy(z, zr.at[0, ds, oth], f_s.at[0, ds], f_r.at[0, ds], core)
        cp.start()
        f_out.append(cp)

    def core_copy(ds, i):
        return rcopy(
            zr.at[1, ds, share(0, rel(i))], zr.at[1, ds, share(1, rel(i))],
            f1_s.at[ds, i], f1_r.at[ds, i], core,
        )

    for i in range(1, N):
        ds = lax.rem(d + i, N)
        z = zr.at[1, ds, share(0, c)]
        rcopy(z, z, z_s.at[1, i], z_r.at[1, ds], {"dp": d}).wait_recv()
        for j in range(1, C):
            cp = rcopy(z, z, xf_s.at[ds, j], xf_r.at[ds, C - j], {"cuts": rel(j)})
            cp.start()
            f_out.append(cp)
        cp = core_copy(ds, 0)
        cp.start()
        f_out.append(cp)
    for kind in range(2):
        z_local(kind, 0).wait()
    wt = 256 if Dq % 256 == 0 else 128

    def weight_grads(ds, first):
        hwt[...] = hz[ds, :, pl.ds(2 * K * W, K * W)].T

        def wstep(t, _):
            at = pl.ds(pl.multiple_of(t * wt, 128), wt)
            full = dot(zr[0, ds, :, at], hz[ds, :, pl.ds(0, 2 * K * W)], 0, 0)
            down = dot(hwt[...], zr[1, ds, :, at], 1, 0)
            for k in range(K):
                for ref, part in (
                    (g_gate.at[k, at, :], full[:, 2 * k * W : (2 * k + 1) * W]),
                    (g_up.at[k, at, :], full[:, (2 * k + 1) * W : (2 * k + 2) * W]),
                    (g_down.at[k, :, at], down[k * W : (k + 1) * W]),
                ):
                    ref[...] = part if first else ref[...] + part
            return 0

        lax.fori_loop(0, Dq // wt, wstep, 0)

    steps = 2 * (N - 1)

    def source(t):
        hop = t // 2 + 1
        up = lax.rem(t, 2) == 0
        ds = jnp.where(up, d - hop, d + hop)
        return up, ds, (ds >= 0) & (ds < N)

    def hops(t, _):
        up, ds, there = source(t)

        @pl.when(there)
        def _():
            for n in range(2):
                at = hz.at[ds, pieces[n]]
                rcopy(at, at, h_s.at[0, ds, n], h_r.at[ds, n], {"dp": d}).wait_recv()

                @pl.when(up & (d < N - 1))
                def _():
                    h_copy(ds, n, True).start()

                @pl.when(jnp.logical_not(up) & (d > 0))
                def _():
                    h_copy(ds, n, False).start()

        return 0

    lax.fori_loop(0, steps, hops, 0)
    weight_grads(d, True)

    def far(t, _):
        _, ds, there = source(t)

        @pl.when(there & (t < steps))
        def _():
            for j in range(1, C):
                z = zr.at[1, ds, share(0, rel(j))]
                rcopy(z, z, xf_s.at[ds, j], xf_r.at[ds, j], {"cuts": c}).wait_recv()
                core_copy(ds, j).start()

        _, before, was = source(t - 2)

        @pl.when(was & (t >= 2))
        def _():
            z = zr.at[0, before, oth]
            rcopy(z, z, f_s.at[0, before], f_r.at[0, before], core).wait_recv()
            for j in range(C):
                core_copy(before, j).wait_recv()
            weight_grads(before, False)

        return 0

    lax.fori_loop(0, steps + 2, far, 0)

    outs = (out_o, grad_o)
    for kind in range(2):
        for r in range(R):
            rcopy(
                csend.at[kind, r], cr.at[kind, r], rc_s.at[kind, r], rc_r.at[kind, r], core
            ).wait_recv()
            total = ploc[kind, r] + cr[kind, r].astype(F32)
            for i in range(1, C):
                n = (i - 1) * R + r
                rcopy(
                    xr.at[kind, n], xr.at[kind, n], rx_s.at[kind, n], rx_r.at[kind, n], {"cuts": c}
                ).wait_recv()
                total = total + xr[kind, n].astype(F32)
            outs[kind][:, pl.ds(r * Dq, Dq)] = total.astype(BF)

    for i in range(C):
        for slot in range(2):
            if i or slot:
                g = ggr.at[slot, i]
                rcopy(g, g, gg_s.at[slot, i], gg_r.at[slot, i], {"cuts": c}).wait_recv()
    gg_o[...] = jnp.sum(ggr[...], axis=1)

    for cp in x_out + c_out + rc_out + rx_out + gg_out + f_out:
        cp.wait_send()
    for kind in range(2):
        for p in range(N):
            @pl.when(quarter(p) != d)
            def _():
                z_copy(kind, p).wait_send()

    def sent(ds, _):
        @pl.when(ds != d)
        def _():
            for j in range(1, C):
                core_copy(ds, j).wait_send()

        for n in range(2):
            @pl.when((ds <= d) & (d < N - 1))
            def _():
                h_copy(ds, n, True).wait_send()

            @pl.when((ds >= d) & (d > 0))
            def _():
                h_copy(ds, n, False).wait_send()

        return 0

    lax.fori_loop(0, N, sent, 0)


def settle_kernel(count, *refs):
    n = len(refs) // 3
    sems = refs[-1]
    loads, stores = [], []
    for i in range(n):
        rows = refs[i].shape[0] // count
        for j in range(count):
            at = pl.ds(j * rows, rows)
            cp = pltpu.make_async_copy(refs[i].at[at], refs[2 * n + i].at[at], sems.at[0, i, j])
            cp.start()
            loads.append((cp, i, j, at))
    for cp, i, j, at in loads:
        cp.wait()
        cp = pltpu.make_async_copy(refs[2 * n + i].at[at], refs[n + i].at[at], sems.at[1, i, j])
        cp.start()
        stores.append(cp)
    for cp in stores:
        cp.wait()


def settle(*arrays):
    n = len(arrays)
    hb = pl.BlockSpec(memory_space=pl.ANY)
    return pl.pallas_call(
        functools.partial(settle_kernel, 2),
        out_shape=tuple(jax.ShapeDtypeStruct(a.shape, a.dtype) for a in arrays),
        in_specs=[hb] * n,
        out_specs=(hb,) * n,
        scratch_shapes=[pltpu.VMEM(a.shape, a.dtype) for a in arrays]
        + [pltpu.SemaphoreType.DMA((2, n, 2))],
        compiler_params=pltpu.CompilerParams(vmem_limit_bytes=62 * 2**20),
    )(*arrays)


def on_device(N, C, tokens, routes, gates, w_gate, w_up, w_down, cotangent):
    K, D, W = w_gate.shape
    rows, Dc = tokens.shape
    R = N // C
    Dq = Dc // R
    e = lax.axis_index("expert")
    lanes = jnp.arange(128, dtype=jnp.int32)
    onehot = (routes[:, :, None] == lanes[None, None, :]) & (lanes < 2 * K)[None, None, :]
    dense = jnp.sum(jnp.where(onehot, gates[:, :, None], 0.0), axis=1)
    low, high = dense, jnp.roll(dense, -K, axis=1)
    aux_own = jnp.where(e == 0, low, high)
    aux_oth = jnp.where(e == 0, high, low)
    DMA = pltpu.SemaphoreType.DMA
    V = pltpu.VMEM
    rows2 = 2 * rows
    vm = pl.BlockSpec(memory_space=pltpu.VMEM)
    hb = pl.BlockSpec(memory_space=pl.ANY)
    out, grad, gg, gg_gate, gg_up, gg_down = pl.pallas_call(
        functools.partial(kernel, N, C),
        out_shape=(
            jax.ShapeDtypeStruct((rows, Dc), BF),
            jax.ShapeDtypeStruct((rows, Dc), BF),
            jax.ShapeDtypeStruct((2, 8, 128), F32),
            jax.ShapeDtypeStruct((K, Dq, W), F32),
            jax.ShapeDtypeStruct((K, Dq, W), F32),
            jax.ShapeDtypeStruct((K, W, Dq), F32),
        ),
        in_specs=[hb] * 7,
        out_specs=(vm,) * 6,
        scratch_shapes=[
            V((D, 2 * K * W), BF),
            V((K * W, D), BF),
            V((2, N, rows2, Dq), BF),
            V((2, N, rows2, Dq), BF),
            V((N, rows2, 3 * K * W), BF),
            V((2, rows, 128), F32),
            V((rows2, 2 * K * W), F32),
            V((rows2, K * W), F32),
            V((rows2, K * W), F32),
            V((2, N, rows, Dq), F32),
            V((2, N, rows, Dq), BF),
            V((2, N, rows, Dq), BF),
            V((2, N - R, rows, Dq), BF),
            V((2, N - R, rows, Dq), BF),
            V((2, 8, 128), F32),
            V((2, C, 8, 128), F32),
            V((K * W, rows2), BF),
            DMA((2 * K + 2,)),
            DMA((2, R)),
            DMA((2, N)),
            DMA((2, N)),
            DMA((2, N)),
            DMA((2, N)),
            DMA,
            DMA,
            DMA((2, N)),
            DMA((2, N)),
            DMA((2,)),
            DMA((2, N)),
            DMA((2, N)),
            DMA((N, C)),
            DMA((N, C)),
            DMA((N, C)),
            DMA((N, C)),
            DMA((2, N, 2)),
            DMA((N, 2)),
            DMA((2, N)),
            DMA((2, N)),
            DMA((2, N - R)),
            DMA((2, N - R)),
            DMA((2, C)),
            DMA((2, C)),
        ],
        compiler_params=pltpu.CompilerParams(
            collective_id=0, has_side_effects=True, vmem_limit_bytes=62 * 2**20
        ),
    )(
        tokens, cotangent, aux_own, aux_oth, w_gate, w_up, w_down.reshape(K * W, D)
    )
    out, grad, gg_gate, gg_up, gg_down = settle(out, grad, gg_gate, gg_up, gg_down)
    mine = gg[0, :K].T
    theirs = gg[1, :K].T
    table = jnp.where(
        e == 0, jnp.concatenate([mine, theirs], 1), jnp.concatenate([theirs, mine], 1)
    )
    hot = routes[:, :, None] == jnp.arange(2 * K, dtype=jnp.int32)[None, None, :]
    gate_grad = jnp.sum(jnp.where(hot, table[:, None, :], 0.0), axis=2)
    return (out, grad, gate_grad, gg_gate, gg_up, gg_down)


def solution(mesh):
    in_specs = (
        P(("groups", "dp", "expert"), "cuts"),
        P(("groups", "dp", "expert"), None),
        P(("groups", "dp", "expert"), None),
        P("expert", None, "cuts"),
        P("expert", None, "cuts"),
        P("expert", "cuts", None),
        P(("groups", "dp", "expert"), "cuts"),
    )
    out_specs = (
        P(("groups", "dp", "expert"), "cuts"),
        P(("groups", "dp", "expert"), "cuts"),
        P(("groups", "dp", "expert"), None),
        P(("groups", "expert"), "dp", "cuts"),
        P(("groups", "expert"), "dp", "cuts"),
        P(("groups", "expert"), "cuts", "dp"),
    )
    return jax.shard_map(
        functools.partial(on_device, mesh.shape["dp"], mesh.shape["cuts"]),
        mesh=mesh, in_specs=in_specs, out_specs=out_specs, check_vma=False,
    )
```

```python
import functools

import jax
import jax.numpy as jnp
from jax import lax
from jax.experimental import pallas as pl
from jax.experimental.pallas import tpu as pltpu
from jax.sharding import PartitionSpec as P

MESH = pl.DeviceIdType.MESH
BF = jnp.bfloat16
F32 = jnp.float32


def dot(a, b, ca, cb):
    return lax.dot_general(a, b, (((ca,), (cb,)), ((), ())), preferred_element_type=F32)


def tile_of(width):
    for tile in (512, 384, 256, 128):
        if width % tile == 0:
            return tile
    return width


def kernel(
    N, C, tok, cot, routes, gates, wg, wu, wd_in,
    out_o, grad_o, gate_o, g_gate, g_up, g_down,
    wgu, wd, xg, zr, hz, aux, auxs, acc, accd, hid, ploc, csend, cr, xsend, xr, ggs, ggr, hwt,
    wsem, osem, xs_s, xs_r, co_s, co_r, au_s, au_r, z_s, z_r, zl, f_s, f_r,
    f1_s, f1_r, xf_s, xf_r, h_s, h_r, rc_s, rc_r, rx_s, rx_r, gg_s, gg_r,
):
    d, e, c = lax.axis_index("dp"), lax.axis_index("expert"), lax.axis_index("cuts")
    other = 1 - e
    rows = tok.shape[0]
    R = N // C
    Dq = tok.shape[1] // R
    ins = (tok, cot)
    K = wg.shape[0]
    W = wg.shape[2]

    def rel(i):
        return lax.rem(c + i, C)

    def quarter(p):
        return rel(p // R) * R + p % R

    def cols(p):
        return pl.ds(pl.multiple_of(quarter(p) * Dq, 128), Dq)

    def rcopy(src, dst, ss, rs, dev):
        return pltpu.make_async_remote_copy(
            src_ref=src, dst_ref=dst, send_sem=ss, recv_sem=rs, device_id=dev, device_id_type=MESH
        )

    barrier = pltpu.get_barrier_semaphore()
    peers = [{"cuts": rel(i)} for i in range(1, C)]
    peers += [{"expert": other, "cuts": rel(i)} for i in range(C)]
    peers += [{"dp": lax.rem(d + i, N)} for i in range(1, N)]
    for peer in peers:
        pl.semaphore_signal(barrier, inc=1, device_id=peer, device_id_type=MESH)
    pl.semaphore_wait(barrier, len(peers))

    own = pl.ds(0, rows)
    oth = pl.ds(rows, rows)
    core = {"expert": other}

    x_out = []
    c_out = []
    loc = []
    for kind in range(2):
        for r in range(R):
            src = ins[kind].at[:, pl.ds(r * Dq, Dq)]
            for i in range(1, C):
                p = (C - i) * R + r
                cp = rcopy(src, xg.at[kind, p, own], xs_s.at[kind, p], xs_r.at[kind, p], {"cuts": rel(i)})
                cp.start()
                x_out.append(cp)
            cp = rcopy(src, xg.at[kind, r, oth], co_s.at[kind, r], co_r.at[kind, r], core)
            cp.start()
            c_out.append(cp)
            cp = pltpu.make_async_copy(src, xg.at[kind, r, own], osem.at[kind, r])
            cp.start()
            loc.append(cp)
    w_loads = []
    for k in range(K):
        for j, w in enumerate((wg, wu)):
            cp = pltpu.make_async_copy(
                w.at[k], wgu.at[:, pl.ds((2 * k + j) * W, W)], wsem.at[2 * k + j]
            )
            cp.start()
            w_loads.append(cp)
    wd_load = pltpu.make_async_copy(wd_in, wd, wsem.at[2 * K])
    wd_load.start()

    hr = rows // C

    def share(slot, cc):
        return pl.ds(pl.multiple_of(slot * rows + cc * hr, 16), hr)

    def z_copy(kind, p):
        part = own if kind == 0 else share(0, c)
        return rcopy(
            xg.at[kind, p, part], zr.at[kind, d, part], z_s.at[kind, p], z_r.at[kind, d],
            {"dp": quarter(p)},
        )

    def dense(index):
        ids = lax.broadcasted_iota(jnp.int32, (8, rows), 0)
        want = ids + index * K
        table = jnp.zeros((8, rows), F32)
        for j in range(2):
            hit = (routes[j : j + 1, :] == want) & (ids < K)
            table = table + jnp.where(hit, gates[j : j + 1, :], 0.0)
        return table

    aux[0] = dense(e)
    auxs[...] = dense(other)
    aux_copy = rcopy(auxs, aux.at[1], au_s, au_r, core)
    aux_copy.start()

    def z_local(kind, p):
        return pltpu.make_async_copy(xg.at[kind, p], zr.at[kind, d], zl.at[kind])

    def z_start(kind, p):
        @pl.when(quarter(p) != d)
        def _():
            z_copy(kind, p).start()

    def arrive(kind, p):
        if p >= R:
            rcopy(
                xg.at[kind, p, own], xg.at[kind, p, own], xs_s.at[kind, p], xs_r.at[kind, p],
                {"cuts": c},
            ).wait_recv()
            cp = rcopy(
                xg.at[kind, p, own], xg.at[kind, p, oth], co_s.at[kind, p], co_r.at[kind, p], core
            )
            cp.start()
            c_out.append(cp)
            z_start(kind, p)
        rcopy(
            xg.at[kind, p, own], xg.at[kind, p, oth], co_s.at[kind, p], co_r.at[kind, p], core
        ).wait_recv()

        @pl.when(quarter(p) == d)
        def _():
            z_local(kind, p).start()

    acc[...] = jnp.zeros_like(acc)
    accd[...] = jnp.zeros_like(accd)
    for kind in range(2):
        for p in range(R):
            loc[kind * R + p].wait()
            z_start(kind, p)
    for p in range(N):
        arrive(0, p)
        if p == 0:
            for cp in w_loads:
                cp.wait()
        acc[...] += dot(xg[0, p], wgu[cols(p), :], 1, 0)
    aux_copy.wait()
    by_token = [jnp.concatenate([aux[n], jnp.zeros((120, rows), F32)], 0).T for n in range(2)]
    wd_load.wait()

    def weight(k):
        return jnp.concatenate([t[:, k : k + 1] for t in by_token], axis=0)

    for k in range(K):
        gs = pl.ds(2 * k * W, W)
        us = pl.ds((2 * k + 1) * W, W)
        g = acc[:, gs]
        u = acc[:, us]
        s = jax.nn.sigmoid(g)
        silu = g * s
        h = silu * u
        w = weight(k)
        hid[:, pl.ds(k * W, W)] = h
        hz[d, :, pl.ds((2 * K + k) * W, W)] = (h * w).astype(BF)
        acc[:, gs] = u * s * (1.0 + g * (1.0 - s)) * w
        acc[:, us] = silu * w

    tile = tile_of(Dq)
    rx_out = []
    rc_out = []

    def back(kind):
        order = list(range(R, N)) + list(range(R))
        for p in order:
            base = quarter(p) * Dq

            def step(t, _, p=p, base=base):
                at = pl.ds(pl.multiple_of(t * tile, 128), tile)
                wat = pl.ds(pl.multiple_of(base + t * tile, 128), tile)
                if kind == 0:
                    part = dot(hz[d, :, pl.ds(2 * K * W, K * W)], wd[:, wat], 1, 0)
                else:
                    part = dot(hz[d, :, pl.ds(0, 2 * K * W)], wgu[wat, :], 1, 1)
                ploc[kind, p, :, at] = part[:rows]
                csend[kind, p, :, at] = part[rows:].astype(BF)
                return 0

            lax.fori_loop(0, Dq // tile, step, 0)
            cp = rcopy(csend.at[kind, p], cr.at[kind, p], rc_s.at[kind, p], rc_r.at[kind, p], core)
            cp.start()
            rc_out.append(cp)
        for p in order[: N - R]:
            rcopy(
                csend.at[kind, p], cr.at[kind, p], rc_s.at[kind, p], rc_r.at[kind, p], core
            ).wait_recv()
            xsend[kind, p - R] = (ploc[kind, p] + cr[kind, p].astype(F32)).astype(BF)
            cp = rcopy(
                xsend.at[kind, p - R], xr.at[kind, p - R], rx_s.at[kind, p - R],
                rx_r.at[kind, p - R], {"cuts": rel(p // R)},
            )
            cp.start()
            rx_out.append(cp)

    back(0)

    for p in range(N):
        arrive(1, p)
        accd[...] += dot(xg[1, p], wd[:, cols(p)], 1, 1)

    ggs[...] = jnp.zeros_like(ggs)
    for k in range(K):
        dh = accd[:, pl.ds(k * W, W)]
        prod = hid[:, pl.ds(k * W, W)] * dh
        for slot in range(2):
            piece = prod[slot * rows : (slot + 1) * rows]
            ggs[slot, pl.ds(k, 1), :] = jnp.sum(piece.T, axis=0, keepdims=True)
        hz[d, :, pl.ds(2 * k * W, W)] = (acc[:, pl.ds(2 * k * W, W)] * dh).astype(BF)
        hz[d, :, pl.ds((2 * k + 1) * W, W)] = (acc[:, pl.ds((2 * k + 1) * W, W)] * dh).astype(BF)

    gg_out = []
    for i in range(C):
        for slot in range(2):
            if i == 0 and slot == 0:
                continue
            dev = {"cuts": rel(i)} if slot == 0 else {"expert": other, "cuts": rel(i)}
            cp = rcopy(ggs.at[slot], ggr.at[slot, i], gg_s.at[slot, i], gg_r.at[slot, i], dev)
            cp.start()
            gg_out.append(cp)
    ggr[0, 0] = ggs[0]

    pieces = (own, oth)

    def h_copy(ds, n, up):
        at = hz.at[ds, pieces[n]]
        to = jnp.minimum(d + 1, N - 1) if up else jnp.maximum(d - 1, 0)
        return rcopy(at, at, h_s.at[int(up), ds, n], h_r.at[ds, n], {"dp": to})

    for n in range(2):
        @pl.when(d < N - 1)
        def _():
            h_copy(d, n, True).start()

        @pl.when(d > 0)
        def _():
            h_copy(d, n, False).start()

    back(1)

    f_out = []
    for i in range(1, N):
        ds = lax.rem(d + i, N)
        z = zr.at[0, ds, own]
        rcopy(z, z, z_s.at[0, i], z_r.at[0, ds], {"dp": d}).wait_recv()
        cp = rcopy(z, zr.at[0, ds, oth], f_s.at[0, ds], f_r.at[0, ds], core)
        cp.start()
        f_out.append(cp)

    def core_copy(ds, i):
        return rcopy(
            zr.at[1, ds, share(0, rel(i))], zr.at[1, ds, share(1, rel(i))],
            f1_s.at[ds, i], f1_r.at[ds, i], core,
        )

    for i in range(1, N):
        ds = lax.rem(d + i, N)
        z = zr.at[1, ds, share(0, c)]
        rcopy(z, z, z_s.at[1, i], z_r.at[1, ds], {"dp": d}).wait_recv()
        for j in range(1, C):
            cp = rcopy(z, z, xf_s.at[ds, j], xf_r.at[ds, C - j], {"cuts": rel(j)})
            cp.start()
            f_out.append(cp)
        cp = core_copy(ds, 0)
        cp.start()
        f_out.append(cp)
    for kind in range(2):
        z_local(kind, 0).wait()
    wt = 256 if Dq % 256 == 0 else 128

    def weight_grads(ds, first):
        hwt[...] = hz[ds, :, pl.ds(2 * K * W, K * W)].T

        def wstep(t, _):
            at = pl.ds(pl.multiple_of(t * wt, 128), wt)
            full = dot(zr[0, ds, :, at], hz[ds, :, pl.ds(0, 2 * K * W)], 0, 0)
            down = dot(hwt[...], zr[1, ds, :, at], 1, 0)
            for k in range(K):
                for ref, part in (
                    (g_gate.at[k, at, :], full[:, 2 * k * W : (2 * k + 1) * W]),
                    (g_up.at[k, at, :], full[:, (2 * k + 1) * W : (2 * k + 2) * W]),
                    (g_down.at[k, :, at], down[k * W : (k + 1) * W]),
                ):
                    ref[...] = part if first else ref[...] + part
            return 0

        lax.fori_loop(0, Dq // wt, wstep, 0)

    steps = 2 * (N - 1)

    def source(t):
        hop = t // 2 + 1
        up = lax.rem(t, 2) == 0
        ds = jnp.where(up, d - hop, d + hop)
        return up, ds, (ds >= 0) & (ds < N)

    def hops(t, _):
        up, ds, there = source(t)

        @pl.when(there)
        def _():
            for n in range(2):
                at = hz.at[ds, pieces[n]]
                rcopy(at, at, h_s.at[0, ds, n], h_r.at[ds, n], {"dp": d}).wait_recv()

                @pl.when(up & (d < N - 1))
                def _():
                    h_copy(ds, n, True).start()

                @pl.when(jnp.logical_not(up) & (d > 0))
                def _():
                    h_copy(ds, n, False).start()

        return 0

    outs = (out_o, grad_o)
    def final(kind):
        for r in range(R):
            rcopy(
                csend.at[kind, r], cr.at[kind, r], rc_s.at[kind, r], rc_r.at[kind, r], core
            ).wait_recv()
            total = ploc[kind, r] + cr[kind, r].astype(F32)
            for i in range(1, C):
                n = (i - 1) * R + r
                rcopy(
                    xr.at[kind, n], xr.at[kind, n], rx_s.at[kind, n], rx_r.at[kind, n], {"cuts": c}
                ).wait_recv()
                total = total + xr[kind, n].astype(F32)
            outs[kind][:, pl.ds(r * Dq, Dq)] = total.astype(BF)

    lax.fori_loop(0, steps, hops, 0)
    final(0)
    weight_grads(d, True)

    def far(t, _):
        _, ds, there = source(t)

        @pl.when(there & (t < steps))
        def _():
            for j in range(1, C):
                z = zr.at[1, ds, share(0, rel(j))]
                rcopy(z, z, xf_s.at[ds, j], xf_r.at[ds, j], {"cuts": c}).wait_recv()
                core_copy(ds, j).start()

        _, before, was = source(t - 2)

        @pl.when(was & (t >= 2))
        def _():
            z = zr.at[0, before, oth]
            rcopy(z, z, f_s.at[0, before], f_r.at[0, before], core).wait_recv()
            for j in range(C):
                core_copy(before, j).wait_recv()
            weight_grads(before, False)

        return 0

    lax.fori_loop(0, steps + 2, far, 0)

    final(1)

    for i in range(C):
        for slot in range(2):
            if i or slot:
                g = ggr.at[slot, i]
                rcopy(g, g, gg_s.at[slot, i], gg_r.at[slot, i], {"cuts": c}).wait_recv()
    sums = jnp.sum(ggr[...], axis=1)
    for j in range(2):
        total = jnp.zeros((1, rows), F32)
        for n, index in enumerate((e, other)):
            for k in range(K):
                hit = routes[j : j + 1, :] == index * K + k
                total = total + jnp.where(hit, sums[n, k : k + 1, :], 0.0)
        gate_o[j : j + 1, :] = total

    for cp in x_out + c_out + rc_out + rx_out + gg_out + f_out:
        cp.wait_send()
    for kind in range(2):
        for p in range(N):
            @pl.when(quarter(p) != d)
            def _():
                z_copy(kind, p).wait_send()

    def sent(ds, _):
        @pl.when(ds != d)
        def _():
            for j in range(1, C):
                core_copy(ds, j).wait_send()

        for n in range(2):
            @pl.when((ds <= d) & (d < N - 1))
            def _():
                h_copy(ds, n, True).wait_send()

            @pl.when((ds >= d) & (d > 0))
            def _():
                h_copy(ds, n, False).wait_send()

        return 0

    lax.fori_loop(0, N, sent, 0)


def settle_kernel(count, *refs):
    n = len(refs) // 3
    sems = refs[-1]
    loads, stores = [], []
    for i in range(n):
        parts = 1 if refs[i].shape[0] % count or len(refs[i].shape) == 2 and refs[i].shape[0] < 32 else count
        rows = refs[i].shape[0] // parts
        for j in range(parts):
            at = pl.ds(j * rows, rows)
            cp = pltpu.make_async_copy(refs[i].at[at], refs[2 * n + i].at[at], sems.at[0, i, j])
            cp.start()
            loads.append((cp, i, j, at))
    for cp, i, j, at in loads:
        cp.wait()
        cp = pltpu.make_async_copy(refs[2 * n + i].at[at], refs[n + i].at[at], sems.at[1, i, j])
        cp.start()
        stores.append(cp)
    for cp in stores:
        cp.wait()


def settle(*arrays):
    n = len(arrays)
    hb = pl.BlockSpec(memory_space=pl.ANY)
    return pl.pallas_call(
        functools.partial(settle_kernel, 2),
        out_shape=tuple(jax.ShapeDtypeStruct(a.shape, a.dtype) for a in arrays),
        in_specs=[hb] * n,
        out_specs=(hb,) * n,
        scratch_shapes=[pltpu.VMEM(a.shape, a.dtype) for a in arrays]
        + [pltpu.SemaphoreType.DMA((2, n, 2))],
        compiler_params=pltpu.CompilerParams(vmem_limit_bytes=62 * 2**20),
    )(*arrays)


def on_device(N, C, tokens, routes, gates, w_gate, w_up, w_down, cotangent):
    K, D, W = w_gate.shape
    rows, Dc = tokens.shape
    R = N // C
    Dq = Dc // R
    DMA = pltpu.SemaphoreType.DMA
    V = pltpu.VMEM
    rows2 = 2 * rows
    vm = pl.BlockSpec(memory_space=pltpu.VMEM)
    hb = pl.BlockSpec(memory_space=pl.ANY)
    results = pl.pallas_call(
        functools.partial(kernel, N, C),
        out_shape=(
            jax.ShapeDtypeStruct((rows, Dc), BF),
            jax.ShapeDtypeStruct((rows, Dc), BF),
            jax.ShapeDtypeStruct((2, rows), F32),
            jax.ShapeDtypeStruct((K, Dq, W), F32),
            jax.ShapeDtypeStruct((K, Dq, W), F32),
            jax.ShapeDtypeStruct((K, W, Dq), F32),
        ),
        in_specs=[hb, hb, vm, vm, hb, hb, hb],
        out_specs=(vm,) * 6,
        scratch_shapes=[
            V((D, 2 * K * W), BF),
            V((K * W, D), BF),
            V((2, N, rows2, Dq), BF),
            V((2, N, rows2, Dq), BF),
            V((N, rows2, 3 * K * W), BF),
            V((2, 8, rows), F32),
            V((8, rows), F32),
            V((rows2, 2 * K * W), F32),
            V((rows2, K * W), F32),
            V((rows2, K * W), F32),
            V((2, N, rows, Dq), F32),
            V((2, N, rows, Dq), BF),
            V((2, N, rows, Dq), BF),
            V((2, N - R, rows, Dq), BF),
            V((2, N - R, rows, Dq), BF),
            V((2, 8, 128), F32),
            V((2, C, 8, 128), F32),
            V((K * W, rows2), BF),
            DMA((2 * K + 2,)),
            DMA((2, R)),
            DMA((2, N)),
            DMA((2, N)),
            DMA((2, N)),
            DMA((2, N)),
            DMA,
            DMA,
            DMA((2, N)),
            DMA((2, N)),
            DMA((2,)),
            DMA((2, N)),
            DMA((2, N)),
            DMA((N, C)),
            DMA((N, C)),
            DMA((N, C)),
            DMA((N, C)),
            DMA((2, N, 2)),
            DMA((N, 2)),
            DMA((2, N)),
            DMA((2, N)),
            DMA((2, N - R)),
            DMA((2, N - R)),
            DMA((2, C)),
            DMA((2, C)),
        ],
        compiler_params=pltpu.CompilerParams(
            collective_id=0, has_side_effects=True, vmem_limit_bytes=62 * 2**20
        ),
    )(
        tokens, cotangent, routes.T, gates.T, w_gate, w_up, w_down.reshape(K * W, D)
    )
    out, grad, gate_grad, gg_gate, gg_up, gg_down = settle(*results)
    return (out, grad, gate_grad.T, gg_gate, gg_up, gg_down)


def solution(mesh):
    in_specs = (
        P(("groups", "dp", "expert"), "cuts"),
        P(("groups", "dp", "expert"), None),
        P(("groups", "dp", "expert"), None),
        P("expert", None, "cuts"),
        P("expert", None, "cuts"),
        P("expert", "cuts", None),
        P(("groups", "dp", "expert"), "cuts"),
    )
    out_specs = (
        P(("groups", "dp", "expert"), "cuts"),
        P(("groups", "dp", "expert"), "cuts"),
        P(("groups", "dp", "expert"), None),
        P(("groups", "expert"), "dp", "cuts"),
        P(("groups", "expert"), "dp", "cuts"),
        P(("groups", "expert"), "cuts", "dp"),
    )
    return jax.shard_map(
        functools.partial(on_device, mesh.shape["dp"], mesh.shape["cuts"]),
        mesh=mesh, in_specs=in_specs, out_specs=out_specs, check_vma=False,
    )
```

```python
import functools

import jax
import jax.numpy as jnp
from jax import lax
from jax.experimental import pallas as pl
from jax.experimental.pallas import tpu as pltpu
from jax.sharding import PartitionSpec as P

MESH = pl.DeviceIdType.MESH
BF = jnp.bfloat16
F32 = jnp.float32


def dot(a, b, ca, cb):
    return lax.dot_general(a, b, (((ca,), (cb,)), ((), ())), preferred_element_type=F32)


def tile_of(width):
    for tile in (512, 384, 256, 128):
        if width % tile == 0:
            return tile
    return width


def kernel(
    N, C, tok, cot, routes, gates, wg, wu, wd_in,
    out_o, grad_o, gate_o, g_gate, g_up, g_down,
    wgu, wd, xg, zr, hz, aux, auxs, acc, accd, hid, ploc, csend, cr, xsend, xr, ggs, ggr, hwt,
    wsem, osem, xs_s, xs_r, co_s, co_r, au_s, au_r, z_s, z_r, zl, f_s, f_r,
    f1_s, f1_r, xf_s, xf_r, h_s, h_r, rc_s, rc_r, rx_s, rx_r, gg_s, gg_r,
):
    d, e, c = lax.axis_index("dp"), lax.axis_index("expert"), lax.axis_index("cuts")
    other = 1 - e
    rows = tok.shape[0]
    R = N // C
    Dq = tok.shape[1] // R
    ins = (tok, cot)
    K = wg.shape[0]
    W = wg.shape[2]

    def rel(i):
        return lax.rem(c + i, C)

    def quarter(p):
        return rel(p // R) * R + p % R

    def cols(p):
        return pl.ds(pl.multiple_of(quarter(p) * Dq, 128), Dq)

    def rcopy(src, dst, ss, rs, dev):
        return pltpu.make_async_remote_copy(
            src_ref=src, dst_ref=dst, send_sem=ss, recv_sem=rs, device_id=dev, device_id_type=MESH
        )

    barrier = pltpu.get_barrier_semaphore()
    peers = [{"cuts": rel(i)} for i in range(1, C)]
    peers += [{"expert": other, "cuts": rel(i)} for i in range(C)]
    peers += [{"dp": lax.rem(d + i, N)} for i in range(1, N)]
    for peer in peers:
        pl.semaphore_signal(barrier, inc=1, device_id=peer, device_id_type=MESH)
    pl.semaphore_wait(barrier, len(peers))

    own = pl.ds(0, rows)
    oth = pl.ds(rows, rows)
    core = {"expert": other}

    x_out = []
    c_out = []
    loc = []
    for kind in range(2):
        for r in range(R):
            src = ins[kind].at[:, pl.ds(r * Dq, Dq)]
            for i in range(1, C):
                p = (C - i) * R + r
                cp = rcopy(src, xg.at[kind, p, own], xs_s.at[kind, p], xs_r.at[kind, p], {"cuts": rel(i)})
                cp.start()
                x_out.append(cp)
            cp = rcopy(src, xg.at[kind, r, oth], co_s.at[kind, r], co_r.at[kind, r], core)
            cp.start()
            c_out.append(cp)
            cp = pltpu.make_async_copy(src, xg.at[kind, r, own], osem.at[kind, r])
            cp.start()
            loc.append(cp)
    w_loads = []
    for k in range(K):
        for j, w in enumerate((wg, wu)):
            cp = pltpu.make_async_copy(
                w.at[k], wgu.at[:, pl.ds((2 * k + j) * W, W)], wsem.at[2 * k + j]
            )
            cp.start()
            w_loads.append(cp)
    wd_load = pltpu.make_async_copy(wd_in, wd, wsem.at[2 * K])
    wd_load.start()

    hr = rows // C

    def share(slot, cc):
        return pl.ds(pl.multiple_of(slot * rows + cc * hr, 16), hr)

    def z_copy(kind, p):
        part = share(0, c) if kind == 0 else own
        return rcopy(
            xg.at[kind, p, part], zr.at[kind, d, part], z_s.at[kind, p], z_r.at[kind, d],
            {"dp": quarter(p)},
        )

    def dense(index):
        ids = lax.broadcasted_iota(jnp.int32, (8, rows), 0)
        want = ids + index * K
        table = jnp.zeros((8, rows), F32)
        for j in range(2):
            hit = (routes[j : j + 1, :] == want) & (ids < K)
            table = table + jnp.where(hit, gates[j : j + 1, :], 0.0)
        return table

    aux[0] = dense(e)
    auxs[...] = dense(other)
    aux_copy = rcopy(auxs, aux.at[1], au_s, au_r, core)
    aux_copy.start()

    def z_local(kind, p):
        return pltpu.make_async_copy(xg.at[kind, p], zr.at[kind, d], zl.at[kind])

    def z_start(kind, p):
        @pl.when(quarter(p) != d)
        def _():
            z_copy(kind, p).start()

    def arrive(kind, p):
        if p >= R:
            rcopy(
                xg.at[kind, p, own], xg.at[kind, p, own], xs_s.at[kind, p], xs_r.at[kind, p],
                {"cuts": c},
            ).wait_recv()
            cp = rcopy(
                xg.at[kind, p, own], xg.at[kind, p, oth], co_s.at[kind, p], co_r.at[kind, p], core
            )
            cp.start()
            c_out.append(cp)
            z_start(kind, p)
        rcopy(
            xg.at[kind, p, own], xg.at[kind, p, oth], co_s.at[kind, p], co_r.at[kind, p], core
        ).wait_recv()

        @pl.when(quarter(p) == d)
        def _():
            z_local(kind, p).start()

    acc[...] = jnp.zeros_like(acc)
    accd[...] = jnp.zeros_like(accd)
    for kind in range(2):
        for p in range(R):
            loc[kind * R + p].wait()
            z_start(kind, p)
    for p in range(N):
        arrive(0, p)
        if p == 0:
            for cp in w_loads:
                cp.wait()
        acc[...] += dot(xg[0, p], wgu[cols(p), :], 1, 0)
    aux_copy.wait()
    by_token = [jnp.concatenate([aux[n], jnp.zeros((120, rows), F32)], 0).T for n in range(2)]
    wd_load.wait()

    def weight(k):
        return jnp.concatenate([t[:, k : k + 1] for t in by_token], axis=0)

    for k in range(K):
        gs = pl.ds(2 * k * W, W)
        us = pl.ds((2 * k + 1) * W, W)
        g = acc[:, gs]
        u = acc[:, us]
        s = jax.nn.sigmoid(g)
        silu = g * s
        h = silu * u
        w = weight(k)
        hid[:, pl.ds(k * W, W)] = h
        hz[d, :, pl.ds((2 * K + k) * W, W)] = (h * w).astype(BF)
        acc[:, gs] = u * s * (1.0 + g * (1.0 - s)) * w
        acc[:, us] = silu * w

    tile = tile_of(Dq)
    rx_out = []
    rc_out = []

    def back(kind):
        order = list(range(R, N)) + list(range(R))
        for p in order:
            base = quarter(p) * Dq

            def step(t, _, p=p, base=base):
                at = pl.ds(pl.multiple_of(t * tile, 128), tile)
                wat = pl.ds(pl.multiple_of(base + t * tile, 128), tile)
                if kind == 0:
                    part = dot(hz[d, :, pl.ds(2 * K * W, K * W)], wd[:, wat], 1, 0)
                else:
                    part = dot(hz[d, :, pl.ds(0, 2 * K * W)], wgu[wat, :], 1, 1)
                ploc[kind, p, :, at] = part[:rows]
                csend[kind, p, :, at] = part[rows:].astype(BF)
                return 0

            lax.fori_loop(0, Dq // tile, step, 0)
            cp = rcopy(csend.at[kind, p], cr.at[kind, p], rc_s.at[kind, p], rc_r.at[kind, p], core)
            cp.start()
            rc_out.append(cp)
        for p in order[: N - R]:
            rcopy(
                csend.at[kind, p], cr.at[kind, p], rc_s.at[kind, p], rc_r.at[kind, p], core
            ).wait_recv()
            xsend[kind, p - R] = (ploc[kind, p] + cr[kind, p].astype(F32)).astype(BF)
            cp = rcopy(
                xsend.at[kind, p - R], xr.at[kind, p - R], rx_s.at[kind, p - R],
                rx_r.at[kind, p - R], {"cuts": rel(p // R)},
            )
            cp.start()
            rx_out.append(cp)

    back(0)

    for p in range(N):
        arrive(1, p)
        accd[...] += dot(xg[1, p], wd[:, cols(p)], 1, 1)

    ggs[...] = jnp.zeros_like(ggs)
    for k in range(K):
        dh = accd[:, pl.ds(k * W, W)]
        prod = hid[:, pl.ds(k * W, W)] * dh
        for slot in range(2):
            piece = prod[slot * rows : (slot + 1) * rows]
            ggs[slot, pl.ds(k, 1), :] = jnp.sum(piece.T, axis=0, keepdims=True)
        hz[d, :, pl.ds(2 * k * W, W)] = (acc[:, pl.ds(2 * k * W, W)] * dh).astype(BF)
        hz[d, :, pl.ds((2 * k + 1) * W, W)] = (acc[:, pl.ds((2 * k + 1) * W, W)] * dh).astype(BF)

    gg_out = []
    for i in range(C):
        for slot in range(2):
            if i == 0 and slot == 0:
                continue
            dev = {"cuts": rel(i)} if slot == 0 else {"expert": other, "cuts": rel(i)}
            cp = rcopy(ggs.at[slot], ggr.at[slot, i], gg_s.at[slot, i], gg_r.at[slot, i], dev)
            cp.start()
            gg_out.append(cp)
    ggr[0, 0] = ggs[0]

    pieces = (own, oth)

    def h_copy(ds, n, up):
        at = hz.at[ds, pieces[n]]
        to = jnp.minimum(d + 1, N - 1) if up else jnp.maximum(d - 1, 0)
        return rcopy(at, at, h_s.at[int(up), ds, n], h_r.at[ds, n], {"dp": to})

    for n in range(2):
        @pl.when(d < N - 1)
        def _():
            h_copy(d, n, True).start()

        @pl.when(d > 0)
        def _():
            h_copy(d, n, False).start()

    f_out = []

    def core_copy(ds, i):
        return rcopy(
            zr.at[0, ds, share(0, rel(i))], zr.at[0, ds, share(1, rel(i))],
            f1_s.at[ds, i], f1_r.at[ds, i], core,
        )

    for i in range(1, N):
        ds = lax.rem(d + i, N)
        z = zr.at[0, ds, share(0, c)]
        rcopy(z, z, z_s.at[0, i], z_r.at[0, ds], {"dp": d}).wait_recv()
        for j in range(1, C):
            cp = rcopy(z, z, xf_s.at[ds, j], xf_r.at[ds, C - j], {"cuts": rel(j)})
            cp.start()
            f_out.append(cp)
        cp = core_copy(ds, 0)
        cp.start()
        f_out.append(cp)

    back(1)

    for i in range(1, N):
        ds = lax.rem(d + i, N)
        z = zr.at[1, ds, own]
        rcopy(z, z, z_s.at[1, i], z_r.at[1, ds], {"dp": d}).wait_recv()
        cp = rcopy(z, zr.at[1, ds, oth], f_s.at[1, ds], f_r.at[1, ds], core)
        cp.start()
        f_out.append(cp)
    for i in range(1, N):
        ds = lax.rem(d + i, N)
        for j in range(1, C):
            z = zr.at[0, ds, share(0, rel(j))]
            rcopy(z, z, xf_s.at[ds, j], xf_r.at[ds, j], {"cuts": c}).wait_recv()
            core_copy(ds, j).start()
    for kind in range(2):
        z_local(kind, 0).wait()
    wt = 256 if Dq % 256 == 0 else 128

    def weight_grads(ds, first):
        hwt[...] = hz[ds, :, pl.ds(2 * K * W, K * W)].T

        def wstep(t, _):
            at = pl.ds(pl.multiple_of(t * wt, 128), wt)
            full = dot(zr[0, ds, :, at], hz[ds, :, pl.ds(0, 2 * K * W)], 0, 0)
            down = dot(hwt[...], zr[1, ds, :, at], 1, 0)
            for k in range(K):
                for ref, part in (
                    (g_gate.at[k, at, :], full[:, 2 * k * W : (2 * k + 1) * W]),
                    (g_up.at[k, at, :], full[:, (2 * k + 1) * W : (2 * k + 2) * W]),
                    (g_down.at[k, :, at], down[k * W : (k + 1) * W]),
                ):
                    ref[...] = part if first else ref[...] + part
            return 0

        lax.fori_loop(0, Dq // wt, wstep, 0)

    steps = 2 * (N - 1)

    def source(t):
        hop = t // 2 + 1
        up = lax.rem(t, 2) == 0
        ds = jnp.where(up, d - hop, d + hop)
        return up, ds, (ds >= 0) & (ds < N)

    def hops(t, _):
        up, ds, there = source(t)

        @pl.when(there)
        def _():
            for n in range(2):
                at = hz.at[ds, pieces[n]]
                rcopy(at, at, h_s.at[0, ds, n], h_r.at[ds, n], {"dp": d}).wait_recv()

                @pl.when(up & (d < N - 1))
                def _():
                    h_copy(ds, n, True).start()

                @pl.when(jnp.logical_not(up) & (d > 0))
                def _():
                    h_copy(ds, n, False).start()

            z = zr.at[1, ds, oth]
            rcopy(z, z, f_s.at[1, ds], f_r.at[1, ds], core).wait_recv()
            for j in range(C):
                core_copy(ds, j).wait_recv()
            weight_grads(ds, False)

        return 0

    outs = (out_o, grad_o)
    def final(kind):
        for r in range(R):
            rcopy(
                csend.at[kind, r], cr.at[kind, r], rc_s.at[kind, r], rc_r.at[kind, r], core
            ).wait_recv()
            total = ploc[kind, r] + cr[kind, r].astype(F32)
            for i in range(1, C):
                n = (i - 1) * R + r
                rcopy(
                    xr.at[kind, n], xr.at[kind, n], rx_s.at[kind, n], rx_r.at[kind, n], {"cuts": c}
                ).wait_recv()
                total = total + xr[kind, n].astype(F32)
            outs[kind][:, pl.ds(r * Dq, Dq)] = total.astype(BF)

    weight_grads(d, True)
    final(0)
    lax.fori_loop(0, steps, hops, 0)

    final(1)

    for i in range(C):
        for slot in range(2):
            if i or slot:
                g = ggr.at[slot, i]
                rcopy(g, g, gg_s.at[slot, i], gg_r.at[slot, i], {"cuts": c}).wait_recv()
    sums = jnp.sum(ggr[...], axis=1)
    for j in range(2):
        total = jnp.zeros((1, rows), F32)
        for n, index in enumerate((e, other)):
            for k in range(K):
                hit = routes[j : j + 1, :] == index * K + k
                total = total + jnp.where(hit, sums[n, k : k + 1, :], 0.0)
        gate_o[j : j + 1, :] = total

    for cp in x_out + c_out + rc_out + rx_out + gg_out + f_out:
        cp.wait_send()
    for kind in range(2):
        for p in range(N):
            @pl.when(quarter(p) != d)
            def _():
                z_copy(kind, p).wait_send()

    def sent(ds, _):
        @pl.when(ds != d)
        def _():
            for j in range(1, C):
                core_copy(ds, j).wait_send()

        for n in range(2):
            @pl.when((ds <= d) & (d < N - 1))
            def _():
                h_copy(ds, n, True).wait_send()

            @pl.when((ds >= d) & (d > 0))
            def _():
                h_copy(ds, n, False).wait_send()

        return 0

    lax.fori_loop(0, N, sent, 0)


def settle_kernel(count, *refs):
    n = len(refs) // 3
    sems = refs[-1]
    loads, stores = [], []
    for i in range(n):
        parts = 1 if refs[i].shape[0] % count or len(refs[i].shape) == 2 and refs[i].shape[0] < 32 else count
        rows = refs[i].shape[0] // parts
        for j in range(parts):
            at = pl.ds(j * rows, rows)
            cp = pltpu.make_async_copy(refs[i].at[at], refs[2 * n + i].at[at], sems.at[0, i, j])
            cp.start()
            loads.append((cp, i, j, at))
    for cp, i, j, at in loads:
        cp.wait()
        cp = pltpu.make_async_copy(refs[2 * n + i].at[at], refs[n + i].at[at], sems.at[1, i, j])
        cp.start()
        stores.append(cp)
    for cp in stores:
        cp.wait()


def settle(*arrays):
    n = len(arrays)
    hb = pl.BlockSpec(memory_space=pl.ANY)
    return pl.pallas_call(
        functools.partial(settle_kernel, 2),
        out_shape=tuple(jax.ShapeDtypeStruct(a.shape, a.dtype) for a in arrays),
        in_specs=[hb] * n,
        out_specs=(hb,) * n,
        scratch_shapes=[pltpu.VMEM(a.shape, a.dtype) for a in arrays]
        + [pltpu.SemaphoreType.DMA((2, n, 2))],
        compiler_params=pltpu.CompilerParams(vmem_limit_bytes=62 * 2**20),
    )(*arrays)


def on_device(N, C, tokens, routes, gates, w_gate, w_up, w_down, cotangent):
    K, D, W = w_gate.shape
    rows, Dc = tokens.shape
    R = N // C
    Dq = Dc // R
    DMA = pltpu.SemaphoreType.DMA
    V = pltpu.VMEM
    rows2 = 2 * rows
    vm = pl.BlockSpec(memory_space=pltpu.VMEM)
    hb = pl.BlockSpec(memory_space=pl.ANY)
    results = pl.pallas_call(
        functools.partial(kernel, N, C),
        out_shape=(
            jax.ShapeDtypeStruct((rows, Dc), BF),
            jax.ShapeDtypeStruct((rows, Dc), BF),
            jax.ShapeDtypeStruct((2, rows), F32),
            jax.ShapeDtypeStruct((K, Dq, W), F32),
            jax.ShapeDtypeStruct((K, Dq, W), F32),
            jax.ShapeDtypeStruct((K, W, Dq), F32),
        ),
        in_specs=[hb, hb, vm, vm, hb, hb, hb],
        out_specs=(vm,) * 6,
        scratch_shapes=[
            V((D, 2 * K * W), BF),
            V((K * W, D), BF),
            V((2, N, rows2, Dq), BF),
            V((2, N, rows2, Dq), BF),
            V((N, rows2, 3 * K * W), BF),
            V((2, 8, rows), F32),
            V((8, rows), F32),
            V((rows2, 2 * K * W), F32),
            V((rows2, K * W), F32),
            V((rows2, K * W), F32),
            V((2, N, rows, Dq), F32),
            V((2, N, rows, Dq), BF),
            V((2, N, rows, Dq), BF),
            V((2, N - R, rows, Dq), BF),
            V((2, N - R, rows, Dq), BF),
            V((2, 8, 128), F32),
            V((2, C, 8, 128), F32),
            V((K * W, rows2), BF),
            DMA((2 * K + 2,)),
            DMA((2, R)),
            DMA((2, N)),
            DMA((2, N)),
            DMA((2, N)),
            DMA((2, N)),
            DMA,
            DMA,
            DMA((2, N)),
            DMA((2, N)),
            DMA((2,)),
            DMA((2, N)),
            DMA((2, N)),
            DMA((N, C)),
            DMA((N, C)),
            DMA((N, C)),
            DMA((N, C)),
            DMA((2, N, 2)),
            DMA((N, 2)),
            DMA((2, N)),
            DMA((2, N)),
            DMA((2, N - R)),
            DMA((2, N - R)),
            DMA((2, C)),
            DMA((2, C)),
        ],
        compiler_params=pltpu.CompilerParams(
            collective_id=0, has_side_effects=True, vmem_limit_bytes=62 * 2**20
        ),
    )(
        tokens, cotangent, routes.T, gates.T, w_gate, w_up, w_down.reshape(K * W, D)
    )
    out, grad, gate_grad, gg_gate, gg_up, gg_down = settle(*results)
    return (out, grad, gate_grad.T, gg_gate, gg_up, gg_down)


def solution(mesh):
    in_specs = (
        P(("groups", "dp", "expert"), "cuts"),
        P(("groups", "dp", "expert"), None),
        P(("groups", "dp", "expert"), None),
        P("expert", None, "cuts"),
        P("expert", None, "cuts"),
        P("expert", "cuts", None),
        P(("groups", "dp", "expert"), "cuts"),
    )
    out_specs = (
        P(("groups", "dp", "expert"), "cuts"),
        P(("groups", "dp", "expert"), "cuts"),
        P(("groups", "dp", "expert"), None),
        P(("groups", "expert"), "dp", "cuts"),
        P(("groups", "expert"), "dp", "cuts"),
        P(("groups", "expert"), "cuts", "dp"),
    )
    return jax.shard_map(
        functools.partial(on_device, mesh.shape["dp"], mesh.shape["cuts"]),
        mesh=mesh, in_specs=in_specs, out_specs=out_specs, check_vma=False,
    )
```
